128 devices in a mesh: row: 16 (over x_lo, y, core), col: 8 (over x_hi, z).
Axes of the slice: x: 4 (x_hi: 2, x_lo: 2; x = x_hi * 2 + x_lo), y: 4, z: 4, core: 2. Of those that a mesh axis runs over, the one named last changes fastest.
Arguments:
- item_embed: float32 [131072, 128], P(('col', 'row')), may hold values from -6 to 6
- item_degree: int32 [131072], P(('col', 'row')), may hold values from 1 to 64
- cotangent: float32 [131072, 128], P(('row', 'col')), may hold values from -6 to 6
- user_degree: int32 [131072], P(('row', 'col')), may hold values from 1 to 64
- tile_values: bfloat16 [128, 384, 128, 128], P(('row', 'col')), may hold values from 0.049804688 to 1
- tile_slots: int32 [128, 384], P(('row', 'col')), may hold values from 0 to 8191, as said below
- tile_count: int32 [128], P(('row', 'col')), may hold values from 48 to 384, as said below
Outputs:
- user_out: float32 [131072, 128], P(('row', 'col'))
- item_grad: float32 [131072, 128], P(('col', 'row'))
The draws below stay inside these ranges and needn't reach their ends.
Inputs may be any that keep to these rules, and one draw needn't show every extreme that they name: `tile_slots`: the 384 slots of one device are distinct. `tile_count`: one device has exactly 384 live slots.
All inputs are finite; a program needn't handle non-finite values.
Results may differ from the reference program's by a relative error of at most 0.0029.
Values may be sent and summed in bfloat16 or wider, within the bound.
No kernel may reach another device: no remote copies, remote signals or barrier semaphores. Data moves between devices by JAX's collectives and lax.ppermute only.
A program may use at most 192 MiB of HBM per device.

```python
import math
import jax
import jax.numpy as jnp
from jax import lax

D = 128
TILE = 128
USER_TILES = 64
ITEM_TILES = 128
TCAP = 384
USERS = 131072
ITEMS = 131072
N_ROW = 16
N_COL = 8


def draw_tile_slots(key, part):
    key = jax.random.fold_in(key, 11)
    keys = jax.random.split(key, N_ROW * N_COL)
    orders = jax.vmap(lambda single: jax.random.permutation(single, USER_TILES * ITEM_TILES))(keys)
    return orders[:, :TCAP].astype(jnp.int32)


def draw_tile_count(key, part):
    key = jax.random.fold_in(key, 23)
    first, second = jax.random.split(key)
    counts = jax.random.randint(first, (N_ROW * N_COL,), TCAP // 8, TCAP // 2 + 1)
    busiest = jax.random.randint(second, (), 0, N_ROW * N_COL)
    place = jnp.arange(N_ROW * N_COL, dtype=jnp.int32)
    return jnp.where(place == busiest, TCAP, counts).astype(jnp.int32)


def place_ends(array, own_key, smallest, high):
    spot = [jax.random.randint(jax.random.fold_in(own_key, axis), (), 0, length) for axis, length in enumerate(array.shape)]
    widest = array.shape.index(max(array.shape))
    next_to = spot[:widest] + [(spot[widest] + 1) % array.shape[widest]] + spot[widest + 1:]
    return array.at[tuple(spot)].set(smallest).at[tuple(next_to)].set(high)


def steps_of(stream_key, extent, shards, least, top_value):
    loudness = 1.0
    for position, parts in shards:
        draws = jax.random.uniform(jax.random.fold_in(jax.random.fold_in(stream_key, 6), position), (parts,), jnp.float32, least / len(shards), top_value / len(shards))
        loudness = loudness * jnp.repeat(jnp.exp(draws), extent[position] // parts).reshape((-1,) + (1,) * (len(extent) - 1 - position))
    return loudness


def centred(stream_key, shape, spread, most, shards=(), kind=jnp.bfloat16):
    factor_of = steps_of(stream_key, shape, shards, -0.22, 0.18) if shards else 1.0
    entries = jax.random.normal(stream_key, shape, jnp.float32) * spread * factor_of
    return jnp.minimum(jnp.maximum(entries, -most), most).astype(kind)


def setup_inputs(seed: int = 0) -> dict:
    splits = jax.random.split(jax.random.key(seed), 8)
    item_embed = centred(splits[0], (ITEMS, D), 1.0, 6.0, ((0, 128),), jnp.float32)
    item_degree = place_ends(jax.random.randint(splits[1], (ITEMS,), 1, 65), jax.random.fold_in(splits[1], 1), 1, 64).astype(jnp.int32)
    cotangent = centred(splits[2], (USERS, D), 1.0, 6.0, ((0, 128),), jnp.float32)
    user_degree = place_ends(jax.random.randint(splits[3], (USERS,), 1, 65), jax.random.fold_in(splits[3], 1), 1, 64).astype(jnp.int32)
    tile_values = jnp.clip(jnp.exp(math.log(1.0) - 2.9996462 * jax.random.uniform(splits[4], (N_ROW * N_COL, TCAP, TILE, TILE), jnp.float32) ** steps_of(splits[4], (N_ROW * N_COL, TCAP, TILE, TILE), ((0, 128),), -0.2, 0.2)), 0.049804688, 1.0).astype(jnp.bfloat16)
    tile_slots = draw_tile_slots(jax.random.fold_in(splits[7], 71), 0)
    tile_count = draw_tile_count(jax.random.fold_in(splits[7], 71), 0)
    return {"item_embed": item_embed, "item_degree": item_degree, "cotangent": cotangent, "user_degree": user_degree, "tile_values": tile_values, "tile_slots": tile_slots, "tile_count": tile_count}


def one_hot_rows(index, count, weight):
    table = (index[None, :] == jnp.arange(count, dtype=jnp.int32)[:, None]).astype(jnp.float32)
    return table * weight[None, :]

def reference(item_embed, item_degree, cotangent, user_degree, tile_values, tile_slots, tile_count):
    inv_item = lax.rsqrt(item_degree.astype(jnp.float32))
    inv_user = lax.rsqrt(user_degree.astype(jnp.float32))
    item_panel = (item_embed * inv_item[:, None]).astype(jnp.bfloat16)
    user_panel = (cotangent * inv_user[:, None]).astype(jnp.bfloat16)
    panel_users = USERS // N_ROW
    panel_items = ITEMS // N_COL

    def visit(carry, inputs):
        user_total, item_total = carry
        values, slot_ids, live_count, device = inputs
        row_index = (device // N_COL).astype(jnp.int32)
        col_index = (device % N_COL).astype(jnp.int32)
        tile_row = (slot_ids // ITEM_TILES).astype(jnp.int32)
        tile_col = (slot_ids % ITEM_TILES).astype(jnp.int32)
        live_mask = (jnp.arange(TCAP, dtype=jnp.int32) < live_count).astype(jnp.float32)
        blocks = values.astype(jnp.float32)
        items_here = lax.dynamic_slice_in_dim(item_panel, (col_index * panel_items).astype(jnp.int32), panel_items, 0)
        items_here = items_here.reshape(ITEM_TILES, TILE, D).astype(jnp.float32)
        users_here = lax.dynamic_slice_in_dim(user_panel, (row_index * panel_users).astype(jnp.int32), panel_users, 0)
        users_here = users_here.reshape(USER_TILES, TILE, D).astype(jnp.float32)
        forward_prod = jnp.einsum('tab,tbd->tad', blocks, items_here[tile_col], precision=lax.Precision.HIGHEST)
        user_part = jnp.dot(one_hot_rows(tile_row, USER_TILES, live_mask), forward_prod.reshape(TCAP, TILE * D), precision=lax.Precision.HIGHEST)
        backward_prod = jnp.einsum('tab,tad->tbd', blocks, users_here[tile_row], precision=lax.Precision.HIGHEST)
        item_part = jnp.dot(one_hot_rows(tile_col, ITEM_TILES, live_mask), backward_prod.reshape(TCAP, TILE * D), precision=lax.Precision.HIGHEST)
        user_start = (row_index * panel_users).astype(jnp.int32)
        item_start = (col_index * panel_items).astype(jnp.int32)
        old_user = lax.dynamic_slice_in_dim(user_total, user_start, panel_users, 0)
        user_total = lax.dynamic_update_slice_in_dim(user_total, old_user + user_part.reshape(panel_users, D), user_start, 0)
        old_item = lax.dynamic_slice_in_dim(item_total, item_start, panel_items, 0)
        item_total = lax.dynamic_update_slice_in_dim(item_total, old_item + item_part.reshape(panel_items, D), item_start, 0)
        return ((user_total, item_total), None)
    start = (jnp.zeros((USERS, D), jnp.float32), jnp.zeros((ITEMS, D), jnp.float32))
    devices = jnp.arange(N_ROW * N_COL, dtype=jnp.int32)
    (user_sum, item_sum), _ = lax.scan(visit, start, (tile_values, tile_slots, tile_count, devices))
    return (user_sum * inv_user[:, None], item_sum * inv_item[:, None])
```

```python
import functools

import jax
import jax.numpy as jnp
from jax import lax
from jax.experimental import pallas as pl
from jax.experimental.pallas import tpu as pltpu
from jax.sharding import PartitionSpec as P

D = 128
TILE = 128
CHUNK = 16
UNROLL = 4


def sparse_kernel(transposed, in_blocks, out_blocks, item_blocks, slots_ref, count_ref, values_ref, panel_ref, out_ref, held, acc, sems):
    slot_total = values_ref.shape[0]
    chunks = slot_total // CHUNK
    live = jnp.minimum(count_ref[0], slot_total)
    used = (live + CHUNK - 1) // CHUNK

    def fetch(j):
        start = pl.multiple_of(j * CHUNK, CHUNK)
        return pltpu.make_async_copy(
            values_ref.at[pl.ds(start, CHUNK)], held.at[pl.ds(start, CHUNK)], sems.at[j]
        )

    def start_chunk(j, carry):
        fetch(j).start()
        return carry

    lax.fori_loop(0, used, start_chunk, 0)
    acc[...] = jnp.zeros_like(acc)

    def visit_chunk(j, carry):
        fetch(j).wait()

        def visit(g, inner):
            base = j * CHUNK + g * UNROLL
            prods, places = [], []
            for u in range(UNROLL):
                k = base + u
                slot = slots_ref[0, k]
                row, col = slot // item_blocks, slot % item_blocks
                source, target = (row, col) if transposed else (col, row)
                tile = held[k]
                block = panel_ref[source]
                left, right = (block, tile) if transposed else (tile, block)
                prods.append(jnp.dot(left, right, preferred_element_type=jnp.float32))
                places.append(jnp.where(k < live, target, out_blocks))
            for prod, place in zip(prods, places):
                acc[place] += prod
            return inner

        return lax.fori_loop(0, CHUNK // UNROLL, visit, carry)

    lax.fori_loop(0, used, visit_chunk, 0)

    def finish(i, carry):
        out_ref[i] = acc[i].astype(out_ref.dtype)
        return carry

    lax.fori_loop(0, out_blocks, finish, 0, unroll=4)


def block_sums(transposed, values, slots, count, panel, out_blocks, item_blocks):
    in_blocks = panel.shape[0]
    slot_total = values.shape[0]
    return pl.pallas_call(
        functools.partial(sparse_kernel, transposed, in_blocks, out_blocks, item_blocks),
        out_shape=jax.ShapeDtypeStruct((out_blocks, TILE, D), jnp.bfloat16),
        in_specs=[
            pl.BlockSpec(memory_space=pltpu.SMEM),
            pl.BlockSpec(memory_space=pltpu.SMEM),
            pl.BlockSpec(memory_space=pl.ANY),
            pl.BlockSpec(memory_space=pltpu.VMEM),
        ],
        out_specs=pl.BlockSpec(memory_space=pltpu.VMEM),
        scratch_shapes=[
            pltpu.VMEM((slot_total, TILE, TILE), jnp.bfloat16),
            pltpu.VMEM((out_blocks + 1, TILE, D), jnp.float32),
            pltpu.SemaphoreType.DMA((slot_total // CHUNK,)),
        ],
        compiler_params=pltpu.CompilerParams(vmem_limit_bytes=50 << 20),
        cost_estimate=pl.CostEstimate(
            flops=8 * slot_total * TILE * TILE * D,
            bytes_accessed=slot_total * TILE * TILE * 2 + (in_blocks + out_blocks) * TILE * D * 2,
            transcendentals=0,
        ),
        name="item_sums" if transposed else "user_sums",
    )(slots, count, values, panel)


def local(item_embed, item_degree, cotangent, user_degree, tile_values, tile_slots, tile_count):
    n_row = lax.axis_size("row")
    n_col = lax.axis_size("col")
    own = item_embed.shape[0] // TILE
    item_blocks = own * n_row
    user_blocks = own * n_col
    values = tile_values[0]
    inv_item = lax.rsqrt(item_degree.astype(jnp.float32))
    inv_user = lax.rsqrt(user_degree.astype(jnp.float32))
    item_panel = (item_embed * inv_item[:, None]).astype(jnp.bfloat16).reshape(own, TILE, D)
    user_panel = (cotangent * inv_user[:, None]).reshape(own, TILE, D)
    user_panel = jnp.swapaxes(user_panel, 1, 2).astype(jnp.bfloat16)
    users_here = lax.all_gather(user_panel, "col", axis=0, tiled=True)
    items_here = lax.all_gather(item_panel, "row", axis=0, tiled=True)
    item_part = block_sums(True, values, tile_slots, tile_count, users_here, item_blocks, item_blocks)
    item_part = lax.all_to_all(item_part, "row", 0, 0, tiled=True)
    user_part = block_sums(False, values, tile_slots, tile_count, items_here, user_blocks, item_blocks)
    user_part = lax.all_to_all(user_part, "col", 0, 0, tiled=True)
    item_sum = jnp.sum(item_part.astype(jnp.float32).reshape(n_row, own, D, TILE), axis=0)
    item_sum = jnp.swapaxes(item_sum, 1, 2).reshape(own * TILE, D)
    user_sum = jnp.sum(user_part.astype(jnp.float32).reshape(n_col, own * TILE, D), axis=0)
    return (user_sum * inv_user[:, None], item_sum * inv_item[:, None])


def solution(mesh):
    in_specs = (
        P(("col", "row"), None),
        P(("col", "row")),
        P(("row", "col"), None),
        P(("row", "col")),
        P(("row", "col"), None, None, None),
        P(("row", "col"), None),
        P(("row", "col")),
    )
    out_specs = (P(("row", "col"), None), P(("col", "row"), None))
    return jax.shard_map(local, mesh=mesh, in_specs=in_specs, out_specs=out_specs, check_vma=False)
```

```python
import functools

import jax
import jax.numpy as jnp
from jax import lax
from jax.experimental import pallas as pl
from jax.experimental.pallas import tpu as pltpu
from jax.sharding import PartitionSpec as P

D = 128
TILE = 128
CHUNK = 24
UNROLL = 24
N_ROW = 16
N_COL = 8
OWN = 8
Z = 4
ORDER = (0, 4, 6, 2, 1, 3, 7, 5)
USER_TILES = OWN * N_COL
ITEM_TILES = OWN * N_ROW


def sparse_kernel(pieces, block_left, out_tiles, plan_ref, count_ref, values_ref, *refs):
    panel_refs, out_refs = refs[:pieces], refs[pieces:pieces + len(out_tiles)]
    held, panel, acc, staged, sems, panel_sems, out_sems = refs[pieces + len(out_tiles):]
    total = sum(out_tiles)
    live = jnp.minimum(count_ref[0], values_ref.shape[0])
    used = (live + CHUNK - 1) // CHUNK
    step = panel.shape[0] // pieces

    def fetch(j):
        start = pl.multiple_of(j * CHUNK, CHUNK)
        return pltpu.make_async_copy(
            values_ref.at[pl.ds(start, CHUNK)], held.at[pl.ds(start, CHUNK)], sems.at[j]
        )

    def fetch_panel(i):
        return pltpu.make_async_copy(
            panel_refs[i], panel.at[pl.ds(i * step, step)], panel_sems.at[i]
        )

    def start_chunk(j, carry):
        fetch(j).start()
        return carry

    for i in range(pieces):
        fetch_panel(i).start()
    lax.fori_loop(0, used, start_chunk, 0)
    acc[...] = jnp.zeros_like(acc)
    for i in range(pieces):
        fetch_panel(i).wait()

    def visit_chunk(j, carry):
        fetch(j).wait()

        def visit(g, inner):
            base = j * CHUNK + g * UNROLL
            prods, places = [], []
            for u in range(UNROLL):
                k = base + u
                tile = held[k]
                block = panel[plan_ref[0, k]]
                left, right = (block, tile) if block_left else (tile, block)
                prods.append(jnp.dot(left, right, preferred_element_type=jnp.float32))
                places.append(plan_ref[1, k])
            for prod, place in zip(prods, places):
                acc[place] += prod
            return inner

        return lax.fori_loop(0, CHUNK // UNROLL, visit, carry)

    lax.fori_loop(0, used, visit_chunk, 0)

    copies, base, stage = [], 0, 0
    for i, (ref, tiles) in enumerate(zip(out_refs, out_tiles)):
        if ref.dtype == acc.dtype:
            source = acc.at[pl.ds(base, tiles)]
            copies.append(pltpu.make_async_copy(source, ref, out_sems.at[i, 0]))
            copies[-1].start()
        base += tiles
    base = 0
    for i, (ref, tiles) in enumerate(zip(out_refs, out_tiles)):
        if ref.dtype != acc.dtype:
            part = min(tiles, 2 * OWN)
            for j in range(tiles // part):
                def finish(t, carry, base=base + j * part, stage=stage):
                    staged[stage + t] = acc[base + t].astype(staged.dtype)
                    return carry

                lax.fori_loop(0, part, finish, 0, unroll=4)
                source = staged.at[pl.ds(stage, part)]
                copies.append(pltpu.make_async_copy(source, ref.at[pl.ds(j * part, part)], out_sems.at[i, j]))
                copies[-1].start()
                stage += part
        base += tiles
    for copy in copies:
        copy.wait()


def by_core(column, core):
    within = (column // (2 * OWN)) * OWN + column % OWN
    other = ((column // OWN) % 2) ^ core
    return within + other * (ITEM_TILES // 2)


def user_plan(slots, count, me_col, core):
    row, column = slots // ITEM_TILES, slots % ITEM_TILES
    owner = (row // OWN) ^ me_col
    group = sum(jnp.where(owner == i, g, 0) for i, g in enumerate(ORDER))
    return plan(by_core(column, core), group * OWN + row % OWN, USER_TILES, count)


def item_plan(slots, count, me_col, core):
    row, column = slots // ITEM_TILES, slots % ITEM_TILES
    return plan(row ^ (me_col * OWN), by_core(column, core), ITEM_TILES, count)


def plan(source, target, out_total, count):
    live = jnp.arange(source.shape[0], dtype=jnp.int32) < count
    return jnp.stack([source, jnp.where(live, target, out_total)]).astype(jnp.int32)


def block_sums(name, block_left, plans, count, values, panels, outs):
    slot_total = values.shape[0]
    pieces = len(panels)
    out_tiles = [shape.shape[0] for shape in outs]
    staged = sum(shape.shape[0] for shape in outs if shape.dtype != jnp.float32)
    panel_tiles = sum(panel.shape[0] for panel in panels)
    return pl.pallas_call(
        functools.partial(sparse_kernel, pieces, block_left, out_tiles),
        out_shape=outs,
        in_specs=[pl.BlockSpec(memory_space=pltpu.SMEM)] * 2 + [pl.BlockSpec(memory_space=pl.ANY)] * (1 + pieces),
        out_specs=[pl.BlockSpec(memory_space=pl.ANY)] * len(outs),
        scratch_shapes=[
            pltpu.VMEM((slot_total, TILE, TILE), jnp.bfloat16),
            pltpu.VMEM((panel_tiles, TILE, D), jnp.bfloat16),
            pltpu.VMEM((sum(out_tiles) + 1, TILE, D), jnp.float32),
            pltpu.VMEM((staged, TILE, D), jnp.bfloat16),
            pltpu.SemaphoreType.DMA((slot_total // CHUNK,)),
            pltpu.SemaphoreType.DMA((pieces,)),
            pltpu.SemaphoreType.DMA((len(outs), max(1, max(out_tiles) // (2 * OWN)))),
        ],
        compiler_params=pltpu.CompilerParams(vmem_limit_bytes=50 << 20),
        cost_estimate=pl.CostEstimate(
            flops=8 * slot_total * TILE * TILE * D,
            bytes_accessed=slot_total * TILE * TILE * 2 + (panel_tiles + sum(out_tiles)) * TILE * D * 2,
            transcendentals=0,
        ),
        name=name,
    )(plans, count, values, *panels)


def exchange(x, axis, k):
    size = lax.axis_size(axis)
    return lax.ppermute(x, axis, [(s, s ^ k) for s in range(size)])


def local(item_embed, item_degree, cotangent, user_degree, tile_values, tile_slots, tile_count):
    me_row, me_col = lax.axis_index("row"), lax.axis_index("col")
    core = me_row % 2
    item_plans = item_plan(tile_slots[0], tile_count[0], me_col, core)
    user_plans = user_plan(tile_slots[0], tile_count[0], me_col, core)
    values = tile_values[0]
    inv_item = lax.rsqrt(item_degree.astype(jnp.float32))
    inv_user = lax.rsqrt(user_degree.astype(jnp.float32))
    item_panel = (item_embed * inv_item[:, None]).astype(jnp.bfloat16).reshape(OWN, TILE, D)
    user_panel = (cotangent * inv_user[:, None]).reshape(OWN, TILE, D)
    user_panel = jnp.swapaxes(user_panel, 1, 2).astype(jnp.bfloat16)
    chips = [[2 * i + core for i in range(N_ROW // 2)] for core in range(2)]
    far = exchange(user_panel, "col", Z)
    item_panel, far = lax.optimization_barrier((item_panel, far))
    spread = jnp.broadcast_to(item_panel[None], (N_ROW // 2, OWN, TILE, D)).reshape(ITEM_TILES // 2, TILE, D)
    items_mine = lax.all_to_all(spread, "row", 0, 0, axis_index_groups=chips, tiled=True)
    items_other = exchange(items_mine, "row", 1)
    near1, near3 = exchange(user_panel, "col", 1), exchange(user_panel, "col", 3)
    far1, far3 = exchange(far, "col", 1), exchange(far, "col", 3)
    near2, far2 = exchange(near3, "col", 1), exchange(far1, "col", 3)
    users = [user_panel, near1, near2, near3, far, far1, far2, far3]
    half = (ITEM_TILES // 2, D, TILE)
    keep, send = block_sums(
        "item_sums", True, item_plans, tile_count, values, users,
        [jax.ShapeDtypeStruct(half, jnp.float32), jax.ShapeDtypeStruct(half, jnp.bfloat16)],
    )
    got = exchange(send, "row", 1)
    items_mine, items_other, keep = lax.optimization_barrier((items_mine, items_other, keep))
    f32, bf16 = jnp.float32, jnp.bfloat16
    own, far_own, a3, b1, a1, b3, a2, b2 = block_sums(
        "user_sums", False, user_plans, tile_count, values, [items_mine, items_other],
        [jax.ShapeDtypeStruct((OWN, TILE, D), dtype) for dtype in [f32] * 4 + [bf16] * 4],
    )
    got, own = lax.optimization_barrier((got, own))
    item_part = (keep + got.astype(jnp.float32)).astype(jnp.bfloat16)
    item_part = lax.all_to_all(item_part, "row", 0, 0, axis_index_groups=chips, tiled=True)
    a2, b2 = exchange(a2, "col", 1), exchange(b2, "col", 3)
    a1, b3 = exchange(a1, "col", 1), exchange(b3, "col", 3)
    b1 = exchange((b1 + b2.astype(f32)).astype(bf16), "col", 1)
    a3 = exchange((a3 + a2.astype(f32)).astype(bf16), "col", 3)
    across = (far_own + b3.astype(f32) + b1.astype(f32)).astype(bf16)
    across = exchange(across, "col", Z)
    item_part, own = lax.optimization_barrier((item_part, own))
    item_sum = jnp.sum(item_part.astype(jnp.float32).reshape(N_ROW // 2, OWN, D, TILE), axis=0)
    item_sum = jnp.swapaxes(item_sum, 1, 2).reshape(OWN * TILE, D)
    user_sum = own + a1.astype(f32) + a3.astype(f32) + across.astype(f32)
    user_sum = user_sum.reshape(OWN * TILE, D)
    return (user_sum * inv_user[:, None], item_sum * inv_item[:, None])


def solution(mesh):
    in_specs = (
        P(("col", "row"), None),
        P(("col", "row")),
        P(("row", "col"), None),
        P(("row", "col")),
        P(("row", "col"), None, None, None),
        P(("row", "col"), None),
        P(("row", "col")),
    )
    out_specs = (P(("row", "col"), None), P(("col", "row"), None))
    return jax.shard_map(local, mesh=mesh, in_specs=in_specs, out_specs=out_specs, check_vma=False)
```

```python
import functools

import jax
import jax.numpy as jnp
from jax import lax
from jax.experimental import pallas as pl
from jax.experimental.pallas import tpu as pltpu
from jax.sharding import PartitionSpec as P

D = 128
TILE = 128
CHUNK = 24
ITEM_COST = 8
USER_COST = 8
UNROLL = 24
N_ROW = 16
N_COL = 8
OWN = 8
Z = 4
ORDER = (0, 4, 6, 2, 1, 3, 7, 5)
USER_TILES = OWN * N_COL
ITEM_TILES = OWN * N_ROW


def sparse_kernel(pieces, block_left, out_tiles, plan_ref, count_ref, values_ref, *refs):
    panel_refs, out_refs = refs[:pieces], refs[pieces:pieces + len(out_tiles)]
    held, panel, acc, staged, sems, panel_sems, out_sems = refs[pieces + len(out_tiles):]
    total = sum(out_tiles)
    live = jnp.minimum(count_ref[0], values_ref.shape[0])
    used = (live + CHUNK - 1) // CHUNK
    step = panel.shape[0] // pieces

    def fetch(j):
        start = pl.multiple_of(j * CHUNK, CHUNK)
        return pltpu.make_async_copy(
            values_ref.at[pl.ds(start, CHUNK)], held.at[pl.ds(start, CHUNK)], sems.at[j]
        )

    def fetch_panel(i):
        return pltpu.make_async_copy(
            panel_refs[i], panel.at[pl.ds(i * step, step)], panel_sems.at[i]
        )

    def start_chunk(j, carry):
        fetch(j).start()
        return carry

    for i in range(pieces):
        fetch_panel(i).start()
    lax.fori_loop(0, used, start_chunk, 0)
    acc[...] = jnp.zeros_like(acc)
    for i in range(pieces):
        fetch_panel(i).wait()

    def visit_chunk(j, carry):
        fetch(j).wait()

        def visit(g, inner):
            base = j * CHUNK + g * UNROLL
            prods, places = [], []
            for u in range(UNROLL):
                k = base + u
                tile = held[k]
                block = panel[plan_ref[0, k]]
                left, right = (block, tile) if block_left else (tile, block)
                prods.append(jnp.dot(left, right, preferred_element_type=jnp.float32))
                places.append(plan_ref[1, k])
            for prod, place in zip(prods, places):
                acc[place] += prod
            return inner

        return lax.fori_loop(0, CHUNK // UNROLL, visit, carry)

    lax.fori_loop(0, used, visit_chunk, 0)

    copies, base, stage = [], 0, 0
    for i, (ref, tiles) in enumerate(zip(out_refs, out_tiles)):
        if ref.dtype == acc.dtype:
            source = acc.at[pl.ds(base, tiles)]
            copies.append(pltpu.make_async_copy(source, ref, out_sems.at[i, 0]))
            copies[-1].start()
        base += tiles
    base = 0
    for i, (ref, tiles) in enumerate(zip(out_refs, out_tiles)):
        if ref.dtype != acc.dtype:
            part = min(tiles, 2 * OWN)
            for j in range(tiles // part):
                def finish(t, carry, base=base + j * part, stage=stage):
                    staged[stage + t] = acc[base + t].astype(staged.dtype)
                    return carry

                lax.fori_loop(0, part, finish, 0, unroll=4)
                source = staged.at[pl.ds(stage, part)]
                copies.append(pltpu.make_async_copy(source, ref.at[pl.ds(j * part, part)], out_sems.at[i, j]))
                copies[-1].start()
                stage += part
        base += tiles
    for copy in copies:
        copy.wait()


def by_core(column, core):
    within = (column // (2 * OWN)) * OWN + column % OWN
    other = ((column // OWN) % 2) ^ core
    return within + other * (ITEM_TILES // 2)


def user_plan(slots, count, me_col, core):
    row, column = slots // ITEM_TILES, slots % ITEM_TILES
    owner = (row // OWN) ^ me_col
    group = sum(jnp.where(owner == i, g, 0) for i, g in enumerate(ORDER))
    return plan(by_core(column, core), group * OWN + row % OWN, USER_TILES, count)


def item_plan(slots, count, me_col, core):
    row, column = slots // ITEM_TILES, slots % ITEM_TILES
    return plan(row ^ (me_col * OWN), by_core(column, core), ITEM_TILES, count)


def plan(source, target, out_total, count):
    live = jnp.arange(source.shape[0], dtype=jnp.int32) < count
    return jnp.stack([source, jnp.where(live, target, out_total)]).astype(jnp.int32)


def block_sums(name, cost, block_left, plans, count, values, panels, outs):
    slot_total = values.shape[0]
    pieces = len(panels)
    out_tiles = [shape.shape[0] for shape in outs]
    staged = sum(shape.shape[0] for shape in outs if shape.dtype != jnp.float32)
    panel_tiles = sum(panel.shape[0] for panel in panels)
    return pl.pallas_call(
        functools.partial(sparse_kernel, pieces, block_left, out_tiles),
        out_shape=outs,
        in_specs=[pl.BlockSpec(memory_space=pltpu.SMEM)] * 2 + [pl.BlockSpec(memory_space=pltpu.HBM)] + [pl.BlockSpec(memory_space=pl.ANY)] * pieces,
        out_specs=[pl.BlockSpec(memory_space=pl.ANY)] * len(outs),
        scratch_shapes=[
            pltpu.VMEM((slot_total, TILE, TILE), jnp.bfloat16),
            pltpu.VMEM((panel_tiles, TILE, D), jnp.bfloat16),
            pltpu.VMEM((sum(out_tiles) + 1, TILE, D), jnp.float32),
            pltpu.VMEM((staged, TILE, D), jnp.bfloat16),
            pltpu.SemaphoreType.DMA((slot_total // CHUNK,)),
            pltpu.SemaphoreType.DMA((pieces,)),
            pltpu.SemaphoreType.DMA((len(outs), max(1, max(out_tiles) // (2 * OWN)))),
        ],
        compiler_params=pltpu.CompilerParams(vmem_limit_bytes=50 << 20),
        cost_estimate=pl.CostEstimate(
            flops=cost * slot_total * TILE * TILE * D,
            bytes_accessed=1 << 20,
            transcendentals=0,
        ),
        name=name,
    )(plans, count, values, *panels)


def exchange(x, axis, k):
    size = lax.axis_size(axis)
    return lax.ppermute(x, axis, [(s, s ^ k) for s in range(size)])


def local(item_embed, item_degree, cotangent, user_degree, tile_values, tile_slots, tile_count):
    me_row, me_col = lax.axis_index("row"), lax.axis_index("col")
    core = me_row % 2
    item_plans = item_plan(tile_slots[0], tile_count[0], me_col, core)
    user_plans = user_plan(tile_slots[0], tile_count[0], me_col, core)
    values = tile_values[0]
    inv_item = lax.rsqrt(item_degree.astype(jnp.float32))
    inv_user = lax.rsqrt(user_degree.astype(jnp.float32))
    user_panel = (cotangent * inv_user[:, None]).reshape(OWN, TILE, D)
    user_panel = jnp.swapaxes(user_panel, 1, 2).astype(jnp.bfloat16)
    chips = [[2 * i + core for i in range(N_ROW // 2)] for core in range(2)]
    item_panel = (item_embed * inv_item[:, None]).astype(jnp.bfloat16).reshape(OWN, TILE, D)
    far = exchange(user_panel, "col", Z)
    near1, near3 = exchange(user_panel, "col", 1), exchange(user_panel, "col", 3)
    spread = jnp.broadcast_to(item_panel[None], (N_ROW // 2, OWN, TILE, D)).reshape(ITEM_TILES // 2, TILE, D)
    far, near1, near3, spread = lax.optimization_barrier((far, near1, near3, spread))
    items_mine = lax.all_to_all(spread, "row", 0, 0, axis_index_groups=chips, tiled=True)
    far1, far3 = exchange(far, "col", 1), exchange(far, "col", 3)
    near2, far2 = exchange(near3, "col", 1), exchange(far1, "col", 3)
    users = [user_panel, near1, near2, near3, far, far1, far2, far3]
    half = (ITEM_TILES // 2, D, TILE)
    keep, send = block_sums(
        "item_sums", ITEM_COST, True, item_plans, tile_count, values, users,
        [jax.ShapeDtypeStruct(half, jnp.bfloat16)] * 2,
    )
    got = exchange(send, "row", 1)
    items_mine, keep = lax.optimization_barrier((items_mine, keep))
    items_other = exchange(items_mine, "row", 1)
    item_part = (keep.astype(jnp.float32) + got.astype(jnp.float32)).astype(jnp.bfloat16)
    items_mine, items_other, item_part = lax.optimization_barrier((items_mine, items_other, item_part))
    item_part = lax.all_to_all(item_part, "row", 0, 0, axis_index_groups=chips, tiled=True)
    f32, bf16 = jnp.float32, jnp.bfloat16
    own, far_own, a3, b1, a1, b3, a2, b2 = block_sums(
        "user_sums", USER_COST, False, user_plans, tile_count, values, [items_mine, items_other],
        [jax.ShapeDtypeStruct((OWN, TILE, D), dtype) for dtype in [f32] * 4 + [bf16] * 4],
    )
    a2, b2 = exchange(a2, "col", 1), exchange(b2, "col", 3)
    a1, b3 = exchange(a1, "col", 1), exchange(b3, "col", 3)
    b1 = exchange((b1 + b2.astype(f32)).astype(bf16), "col", 1)
    a3 = exchange((a3 + a2.astype(f32)).astype(bf16), "col", 3)
    across = (far_own + b3.astype(f32) + b1.astype(f32)).astype(bf16)
    across = exchange(across, "col", Z)
    item_part, own = lax.optimization_barrier((item_part, own))
    item_sum = jnp.sum(item_part.astype(jnp.float32).reshape(N_ROW // 2, OWN, D, TILE), axis=0)
    item_sum = jnp.swapaxes(item_sum, 1, 2).reshape(OWN * TILE, D)
    item_grad = item_sum * inv_item[:, None]
    flat = (OWN * TILE, D)
    scale = jnp.broadcast_to(inv_user[:, None], flat)
    near = (own.reshape(flat) + a1.reshape(flat).astype(f32) + a3.reshape(flat).astype(f32)) * inv_user[:, None]
    across, item_grad, near, scale = lax.optimization_barrier((across, item_grad, near, scale))
    return (near + across.reshape(flat).astype(f32) * scale, item_grad)


def solution(mesh):
    in_specs = (
        P(("col", "row"), None),
        P(("col", "row")),
        P(("row", "col"), None),
        P(("row", "col")),
        P(("row", "col"), None, None, None),
        P(("row", "col"), None),
        P(("row", "col")),
    )
    out_specs = (P(("row", "col"), None), P(("col", "row"), None))
    return jax.shard_map(local, mesh=mesh, in_specs=in_specs, out_specs=out_specs, check_vma=False)
```

```python
import functools

import jax
import jax.numpy as jnp
from jax import lax
from jax.experimental import pallas as pl
from jax.experimental.pallas import tpu as pltpu
from jax.sharding import PartitionSpec as P

D = 128
TILE = 128
CHUNK = 24
ITEM_COST = 12
USER_COST = 8
UNROLL = 24
N_ROW = 16
N_COL = 8
OWN = 8
Z = 4
ORDER = (0, 4, 6, 2, 1, 3, 7, 5)
USER_TILES = OWN * N_COL
ITEM_TILES = OWN * N_ROW


def sparse_kernel(pieces, block_left, out_tiles, plan_ref, count_ref, values_ref, *refs):
    panel_refs, out_refs = refs[:pieces], refs[pieces:pieces + len(out_tiles)]
    held, panel, acc, staged, sems, panel_sems, out_sems = refs[pieces + len(out_tiles):]
    total = sum(out_tiles)
    live = jnp.minimum(count_ref[0], values_ref.shape[0])
    used = (live + CHUNK - 1) // CHUNK
    step = panel.shape[0] // pieces

    def fetch(j):
        start = pl.multiple_of(j * CHUNK, CHUNK)
        return pltpu.make_async_copy(
            values_ref.at[pl.ds(start, CHUNK)], held.at[pl.ds(start, CHUNK)], sems.at[j]
        )

    def fetch_panel(i):
        return pltpu.make_async_copy(
            panel_refs[i], panel.at[pl.ds(i * step, step)], panel_sems.at[i]
        )

    def start_chunk(j, carry):
        fetch(j).start()
        return carry

    for i in range(pieces):
        fetch_panel(i).start()
    lax.fori_loop(0, used, start_chunk, 0)
    acc[...] = jnp.zeros_like(acc)
    for i in range(pieces):
        fetch_panel(i).wait()

    def visit_chunk(j, carry):
        fetch(j).wait()

        def visit(g, inner):
            base = j * CHUNK + g * UNROLL
            prods, places = [], []
            for u in range(UNROLL):
                k = base + u
                tile = held[k]
                block = panel[plan_ref[0, k]]
                left, right = (block, tile) if block_left else (tile, block)
                prods.append(jnp.dot(left, right, preferred_element_type=jnp.float32))
                places.append(plan_ref[1, k])
            for prod, place in zip(prods, places):
                acc[place] += prod
            return inner

        return lax.fori_loop(0, CHUNK // UNROLL, visit, carry)

    lax.fori_loop(0, used, visit_chunk, 0)

    copies, base, stage = [], 0, 0
    for i, (ref, tiles) in enumerate(zip(out_refs, out_tiles)):
        if ref.dtype == acc.dtype:
            source = acc.at[pl.ds(base, tiles)]
            copies.append(pltpu.make_async_copy(source, ref, out_sems.at[i, 0]))
            copies[-1].start()
        base += tiles
    base = 0
    for i, (ref, tiles) in enumerate(zip(out_refs, out_tiles)):
        if ref.dtype != acc.dtype:
            part = min(tiles, 2 * OWN)
            for j in range(tiles // part):
                def finish(t, carry, base=base + j * part, stage=stage):
                    staged[stage + t] = acc[base + t].astype(staged.dtype)
                    return carry

                lax.fori_loop(0, part, finish, 0, unroll=4)
                source = staged.at[pl.ds(stage, part)]
                copies.append(pltpu.make_async_copy(source, ref.at[pl.ds(j * part, part)], out_sems.at[i, j]))
                copies[-1].start()
                stage += part
        base += tiles
    for copy in copies:
        copy.wait()


def by_core(column, core):
    within = (column // (2 * OWN)) * OWN + column % OWN
    other = ((column // OWN) % 2) ^ core
    return within + other * (ITEM_TILES // 2)


def user_plan(slots, count, me_col, core):
    row, column = slots // ITEM_TILES, slots % ITEM_TILES
    owner = (row // OWN) ^ me_col
    group = sum(jnp.where(owner == i, g, 0) for i, g in enumerate(ORDER))
    return plan(by_core(column, core), group * OWN + row % OWN, USER_TILES, count)


def item_plan(slots, count, me_col, core):
    row, column = slots // ITEM_TILES, slots % ITEM_TILES
    return plan(row ^ (me_col * OWN), by_core(column, core), ITEM_TILES, count)


def plan(source, target, out_total, count):
    live = jnp.arange(source.shape[0], dtype=jnp.int32) < count
    return jnp.stack([source, jnp.where(live, target, out_total)]).astype(jnp.int32)


def block_sums(name, cost, block_left, plans, count, values, panels, outs):
    slot_total = values.shape[0]
    pieces = len(panels)
    out_tiles = [shape.shape[0] for shape in outs]
    staged = sum(shape.shape[0] for shape in outs if shape.dtype != jnp.float32)
    panel_tiles = sum(panel.shape[0] for panel in panels)
    return pl.pallas_call(
        functools.partial(sparse_kernel, pieces, block_left, out_tiles),
        out_shape=outs,
        in_specs=[pl.BlockSpec(memory_space=pltpu.SMEM)] * 2 + [pl.BlockSpec(memory_space=pltpu.HBM)] + [pl.BlockSpec(memory_space=pl.ANY)] * pieces,
        out_specs=[pl.BlockSpec(memory_space=pl.ANY)] * len(outs),
        scratch_shapes=[
            pltpu.VMEM((slot_total, TILE, TILE), jnp.bfloat16),
            pltpu.VMEM((panel_tiles, TILE, D), jnp.bfloat16),
            pltpu.VMEM((sum(out_tiles) + 1, TILE, D), jnp.float32),
            pltpu.VMEM((staged, TILE, D), jnp.bfloat16),
            pltpu.SemaphoreType.DMA((slot_total // CHUNK,)),
            pltpu.SemaphoreType.DMA((pieces,)),
            pltpu.SemaphoreType.DMA((len(outs), max(1, max(out_tiles) // (2 * OWN)))),
        ],
        compiler_params=pltpu.CompilerParams(vmem_limit_bytes=50 << 20),
        cost_estimate=pl.CostEstimate(
            flops=cost * slot_total * TILE * TILE * D,
            bytes_accessed=1 << 20,
            transcendentals=0,
        ),
        name=name,
    )(plans, count, values, *panels)


def exchange(x, axis, k):
    size = lax.axis_size(axis)
    return lax.ppermute(x, axis, [(s, s ^ k) for s in range(size)])


def local(item_embed, item_degree, cotangent, user_degree, tile_values, tile_slots, tile_count):
    me_row, me_col = lax.axis_index("row"), lax.axis_index("col")
    core = me_row % 2
    item_plans = item_plan(tile_slots[0], tile_count[0], me_col, core)
    user_plans = user_plan(tile_slots[0], tile_count[0], me_col, core)
    values = tile_values[0]
    inv_item = lax.rsqrt(item_degree.astype(jnp.float32))
    inv_user = lax.rsqrt(user_degree.astype(jnp.float32))
    user_panel = (cotangent * inv_user[:, None]).reshape(OWN, TILE, D)
    user_panel = jnp.swapaxes(user_panel, 1, 2).astype(jnp.bfloat16)
    chips = [[2 * i + core for i in range(N_ROW // 2)] for core in range(2)]
    item_panel = (item_embed * inv_item[:, None]).astype(jnp.bfloat16).reshape(OWN, TILE, D)
    far = exchange(user_panel, "col", Z)
    near1, near3 = exchange(user_panel, "col", 1), exchange(user_panel, "col", 3)
    spread = jnp.broadcast_to(item_panel[None], (N_ROW // 2, OWN, TILE, D)).reshape(ITEM_TILES // 2, TILE, D)
    far, near1, near3, spread = lax.optimization_barrier((far, near1, near3, spread))
    items_mine = lax.all_to_all(spread, "row", 0, 0, axis_index_groups=chips, tiled=True)
    far1, far3 = exchange(far, "col", 1), exchange(far, "col", 3)
    near2, far2 = exchange(near3, "col", 1), exchange(far1, "col", 3)
    users = [user_panel, near1, near2, near3, far, far1, far2, far3]
    half = (ITEM_TILES // 2, D, TILE)
    keep, send = block_sums(
        "item_sums", ITEM_COST, True, item_plans, tile_count, values, users,
        [jax.ShapeDtypeStruct(half, jnp.bfloat16)] * 2,
    )
    got = exchange(send, "row", 1)
    items_mine, keep = lax.optimization_barrier((items_mine, keep))
    items_other = exchange(items_mine, "row", 1)
    item_part = (keep.astype(jnp.float32) + got.astype(jnp.float32)).astype(jnp.bfloat16)
    items_mine, items_other, item_part = lax.optimization_barrier((items_mine, items_other, item_part))
    item_part = lax.all_to_all(item_part, "row", 0, 0, axis_index_groups=chips, tiled=True)
    f32, bf16 = jnp.float32, jnp.bfloat16
    own, far_own, a3, b1, a1, b3, a2, b2 = block_sums(
        "user_sums", USER_COST, False, user_plans, tile_count, values, [items_mine, items_other],
        [jax.ShapeDtypeStruct((OWN, TILE, D), dtype) for dtype in [f32] * 4 + [bf16] * 4],
    )
    a2, b2 = exchange(a2, "col", 1), exchange(b2, "col", 3)
    a1, b3 = exchange(a1, "col", 1), exchange(b3, "col", 3)
    b1 = exchange((b1 + b2.astype(f32)).astype(bf16), "col", 1)
    a3 = exchange((a3 + a2.astype(f32)).astype(bf16), "col", 3)
    across = (far_own + b3.astype(f32) + b1.astype(f32)).astype(bf16)
    across = exchange(across, "col", Z)
    item_part, own = lax.optimization_barrier((item_part, own))
    item_sum = jnp.sum(item_part.astype(jnp.float32).reshape(N_ROW // 2, OWN, D, TILE), axis=0)
    item_sum = jnp.swapaxes(item_sum, 1, 2).reshape(OWN * TILE, D)
    item_grad = item_sum * inv_item[:, None]
    flat = (OWN * TILE, D)
    scale = jnp.broadcast_to(inv_user[:, None], flat)
    near = (own.reshape(flat) + a1.reshape(flat).astype(f32) + a3.reshape(flat).astype(f32)) * inv_user[:, None]
    across, item_grad, near, scale = lax.optimization_barrier((across, item_grad, near, scale))
    return (near + across.reshape(flat).astype(f32) * scale, item_grad)


def solution(mesh):
    in_specs = (
        P(("col", "row"), None),
        P(("col", "row")),
        P(("row", "col"), None),
        P(("row", "col")),
        P(("row", "col"), None, None, None),
        P(("row", "col"), None),
        P(("row", "col")),
    )
    out_specs = (P(("row", "col"), None), P(("col", "row"), None))
    return jax.shard_map(local, mesh=mesh, in_specs=in_specs, out_specs=out_specs, check_vma=False)
```
